128 devices in a mesh: inst: 16 (over y, x), tp: 8 (over z, core).
Axes of the slice: x: 4, y: 4, z: 4, core: 2. Of those that a mesh axis runs over, the one named last changes fastest.
Arguments:
- queries: bfloat16 [4, 128, 128], P(None, 'tp'), may hold values from -100 to 100
- kv_cache: bfloat16 [512, 2, 8, 512, 128], P('inst', None, 'tp'), may hold values from -36 to 36
- slot_meta: int32 [512, 2], P('inst'), may hold values from 0 to 255, as said below
- row_len: int32 [4], replicated, may hold values from 1 to 131072, as said below
- new_slot: int32 [512], P('inst'), may hold values from 0 to 511, as said below
- master: int32 [4], replicated, may hold values from 0 to 15
Outputs:
- moved_cache: bfloat16 [512, 2, 8, 512, 128], P('inst', None, 'tp')
- moved_meta: int32 [512, 2], P('inst')
- attended: float32 [16, 4, 128, 128], P('inst', None, 'tp')
The draws below stay inside these ranges and needn't reach their ends.
Inputs may be any that keep to these rules, and one draw needn't show every extreme that they name: new_slot is a permutation of the slots; slot j of an instance moves to slot j of some instance; slots 2k and 2k+1 of an instance move to the same instance, and every instance sends exactly 2 blocks to every instance. `slot_meta`: every sequence has one or more slots; its slots hold its block numbers 0, 1, ... once each; no sequence has more than 256 slots, and one sequence has exactly that many. `row_len`: a sequence with n slots has more than (n - 1) * 512 and at most n * 512 cached tokens; the sequence with 256 slots has exactly 131072.
All inputs are finite; a program needn't handle non-finite values.
Results may differ from the reference program's by a relative error of at most 0.001.
Values may be sent and summed in bfloat16 or wider, within the bound.
No kernel may reach another device: no remote copies, remote signals or barrier semaphores. Data moves between devices by JAX's collectives and lax.ppermute only.
A program may use at most 128 MiB of HBM per device.

```python
import jax
import jax.numpy as jnp

QH = 128
KVH = 8
HD = 128
BLK = 512
ROWS = 4
SLOTS = 32
G = 16
NBLK = 512
N_INST = 16


def block_layout(key):
    base = jax.random.fold_in(key, 101)
    key_cut, key_place, key_tail, key_rows = jax.random.split(base, 4)
    longest = NBLK // 2
    rest = NBLK - longest
    cuts = jnp.sort(jax.random.permutation(key_cut, rest - 1)[:ROWS - 2] + 1).astype(jnp.int32)
    edges = jnp.concatenate([jnp.zeros((1,), jnp.int32), cuts, jnp.full((1,), rest, jnp.int32)])
    rest_counts = edges[1:] - edges[:-1]
    ordered = jnp.concatenate([jnp.full((1,), longest, jnp.int32), rest_counts])
    counts = ordered[jax.random.permutation(key_rows, ROWS)].astype(jnp.int32)
    ends = jnp.cumsum(counts).astype(jnp.int32)
    starts = ends - counts
    index = jnp.arange(NBLK, dtype=jnp.int32)
    row_of = jnp.sum((index[:, None] >= ends[None, :]).astype(jnp.int32), axis=1)
    pos_of = index - starts[row_of]
    place = jax.random.permutation(key_place, NBLK)
    meta = jnp.stack([row_of[place], pos_of[place]], axis=1).astype(jnp.int32)
    tail = jax.random.randint(key_tail, (ROWS,), 1, BLK + 1)
    tail = jnp.where(counts == longest, BLK, tail)
    lengths = ((counts - 1) * BLK + tail).astype(jnp.int32)
    return (meta, lengths)


def cache_values(key, spread):
    base = jax.random.fold_in(key, 202)
    key_main, key_tok, key_vtok, key_chan = jax.random.split(base, 4)
    raw = jnp.clip(jax.random.normal(key_main, (NBLK, 2, KVH, BLK, HD), jnp.float32), -4.0, 4.0)
    tok_scale = jnp.exp(jax.random.uniform(key_tok, (NBLK, 1, KVH, BLK, 1), jnp.float32, -jnp.log(spread), jnp.log(spread) + 1e-06))
    first_two = jnp.arange(BLK)[None, None, None, :, None] < 2
    tok_scale = jnp.where(first_two, 1.0, tok_scale)
    vtok = jnp.exp(jax.random.uniform(key_vtok, (NBLK, 1, KVH, BLK, 1), jnp.float32, jnp.log(0.3), jnp.log(3.0)))
    vchan = jnp.exp(jax.random.uniform(key_chan, (1, 1, KVH, 1, HD), jnp.float32, jnp.log(0.3), jnp.log(3.0)))
    keys = raw[:, 0:1] * tok_scale
    twin_row = keys[:, :, :, 1:2]
    keys = jnp.concatenate([keys[:, :, :, 0:1], twin_row, keys[:, :, :, 2:]], axis=3)
    values = raw[:, 1:2] * vtok * vchan
    return jnp.concatenate([keys, values], axis=1)


def draw_slot_meta(key, part):
    meta, lengths = block_layout(key)
    return meta


def draw_row_len(key, part):
    meta, lengths = block_layout(key)
    return lengths


def draw_kv_cache(key, part):
    cache = cache_values(key, 1.0)
    return cache.astype(jnp.bfloat16)


def draw_queries(key, part):
    own = jax.random.fold_in(key, 5)
    key_q = jax.random.fold_in(own, 0)
    values = jnp.clip(jax.random.normal(key_q, (ROWS, QH, HD), jnp.float32) * 2.0, -8.0, 8.0)
    return values.astype(jnp.bfloat16)


def draw_new_slot(key, part):
    key = jax.random.fold_in(key, 7)
    key_tau, key_rho, key_delta = jax.random.split(key, 3)
    tau = jax.random.permutation(key_tau, N_INST)
    rho = jax.random.permutation(key_rho, N_INST)
    delta = jax.random.permutation(key_delta, N_INST)[:SLOTS // 2]
    source = jnp.arange(N_INST, dtype=jnp.int32)[:, None]
    column = jnp.arange(SLOTS, dtype=jnp.int32)[None, :]
    target = rho[(tau[source] + delta[column // 2]) % N_INST]
    return (target * SLOTS + column).reshape(NBLK).astype(jnp.int32)


def with_ends(array, stream_key, least, largest):
    spot = [jax.random.randint(jax.random.fold_in(stream_key, axis), (), 0, length) for axis, length in enumerate(array.shape)]
    widest = array.shape.index(max(array.shape))
    beside = spot[:widest] + [(spot[widest] + 1) % array.shape[widest]] + spot[widest + 1:]
    return array.at[tuple(spot)].set(least).at[tuple(beside)].set(largest)


def setup_inputs(seed: int = 0) -> dict:
    key_of = jax.random.split(jax.random.key(seed), 7)
    return {
        "queries": draw_queries(jax.random.fold_in(key_of[6], 71), 0),
        "kv_cache": draw_kv_cache(jax.random.fold_in(key_of[6], 71), 0),
        "slot_meta": draw_slot_meta(jax.random.fold_in(key_of[6], 71), 0),
        "row_len": draw_row_len(jax.random.fold_in(key_of[6], 71), 0),
        "new_slot": draw_new_slot(jax.random.fold_in(key_of[6], 71), 0),
        "master": with_ends(jax.random.randint(key_of[5], (ROWS,), 0, N_INST), jax.random.fold_in(key_of[5], 1), 0, N_INST - 1).astype(jnp.int32),
    }


def reference(queries, kv_cache, slot_meta, row_len, new_slot, master):
    moved_cache = jnp.zeros_like(kv_cache).at[new_slot].set(kv_cache)
    moved_meta = jnp.zeros_like(slot_meta).at[new_slot].set(slot_meta)
    owner = slot_meta[:, 0]
    grouped = queries.reshape(ROWS, KVH, G, HD)[owner].astype(jnp.float32)
    keys = kv_cache[:, 0].astype(jnp.float32)
    values = kv_cache[:, 1].astype(jnp.float32)
    scores = jnp.einsum("skgd,sktd->skgt", grouped, keys) * (HD ** -0.5)
    position = slot_meta[:, 1][:, None] * BLK + jnp.arange(BLK, dtype=jnp.int32)[None, :]
    valid = position < row_len[owner][:, None]
    masked = jnp.where(valid[:, None, None, :], scores, jnp.float32(-1e30))
    row_max = jax.ops.segment_max(masked.max(-1), owner, num_segments=ROWS)
    weights = jnp.where(valid[:, None, None, :], jnp.exp(masked - row_max[owner][..., None]), jnp.float32(0.0))
    total = jax.ops.segment_sum(weights.sum(-1), owner, num_segments=ROWS)
    summed = jax.ops.segment_sum(jnp.einsum("skgt,sktd->skgd", weights, values), owner, num_segments=ROWS)
    result = (summed / total[..., None]).reshape(ROWS, KVH * G, HD)
    mine = jnp.arange(N_INST, dtype=jnp.int32)[:, None] == master[None, :]
    attended = jnp.where(mine[:, :, None, None], result[None], jnp.float32(0.0)).astype(jnp.float32)
    return moved_cache, moved_meta, attended
```

```python
import functools

import jax
import jax.numpy as jnp
from jax import lax
from jax.experimental import pallas as pl
from jax.experimental.pallas import tpu as pltpu
from jax.sharding import PartitionSpec as P

LOWEST = -1e30
MAX_LANE, TOTAL_LANE, META_LANE = 0, 32, 64


def gather_pairs(pairs, slots, new_slot_ref, cache_ref, out_ref, sems):
    copies = []
    for k in range(pairs):
        dest = new_slot_ref[2 * k] // slots
        copy = pltpu.make_async_copy(
            cache_ref.at[pl.ds(2 * k, 2)], out_ref.at[pl.ds(2 * dest, 2)], sems.at[k]
        )
        copy.start()
        copies.append(copy)
    for copy in copies:
        copy.wait()


def place_pairs(pairs, place_ref, arrived_ref, out_ref, sems):
    copies = []
    for i in range(pairs):
        copy = pltpu.make_async_copy(
            arrived_ref.at[pl.ds(2 * i, 2)], out_ref.at[pl.ds(2 * place_ref[i], 2)], sems.at[i]
        )
        copy.start()
        copies.append(copy)
    for copy in copies:
        copy.wait()


def attend_kernel(
    slots, group, meta_ref, len_ref, new_slot_ref, q_ref, kv_ref, out_ref, max_ref, total_ref, sum_ref
):
    step = pl.program_id(0)
    rows, heads, width = q_ref.shape
    block = kv_ref.shape[3]
    lane = lax.broadcasted_iota(jnp.int32, (heads, block), 1)
    for j in range(group):
        slot = step * group + j
        row = meta_ref[2 * slot]
        left = len_ref[row] - meta_ref[2 * slot + 1] * block
        scores = lax.dot_general(
            q_ref[row], kv_ref[j, 0, 0], (((1,), (1,)), ((), ())), preferred_element_type=jnp.float32
        ) * width ** (-0.5)
        valid = lane < left
        scores = jnp.where(valid, scores, LOWEST)
        peak = scores.max(-1, keepdims=True)
        weight = jnp.where(valid, jnp.exp(scores - peak), 0.0)
        high = weight.astype(jnp.bfloat16)
        low = (weight - high.astype(jnp.float32)).astype(jnp.bfloat16)
        both = jnp.dot(
            jnp.concatenate([high, low], axis=0), kv_ref[j, 1, 0], preferred_element_type=jnp.float32
        )
        sum_ref[slot] = both[:heads] + both[heads:]
        max_ref[slot] = jnp.broadcast_to(peak, (heads, width))
        total_ref[slot] = jnp.broadcast_to(weight.sum(-1, keepdims=True), (heads, width))

    @pl.when(step == slots // group - 1)
    def _():
        lanes = lax.broadcasted_iota(jnp.int32, (heads, width), 1)
        per = out_ref.shape[1] // 2
        for row in range(rows):
            peak = jnp.full((heads, width), LOWEST, jnp.float32)
            for slot in range(slots):
                peak = jnp.maximum(peak, jnp.where(meta_ref[2 * slot] == row, max_ref[slot], LOWEST))
            total = jnp.zeros((heads, width), jnp.float32)
            summed = jnp.zeros((heads, width), jnp.float32)
            for slot in range(slots):
                scale = jnp.where(meta_ref[2 * slot] == row, jnp.exp(max_ref[slot] - peak), 0.0)
                total = total + scale * total_ref[slot]
                summed = summed + scale * sum_ref[slot]
            stats = jnp.where(lanes < TOTAL_LANE, peak, total)
            for part in range(heads // per):
                dest = row * (heads // per) + part
                out_ref[dest, :per] = summed[part * per : (part + 1) * per]
                out_ref[dest, per:] = stats[part * per : (part + 1) * per]
        lanes = lax.broadcasted_iota(jnp.int32, (per, width), 1)
        for k in range(slots // 2):
            dest = new_slot_ref[2 * k] // slots
            values = [k] + [meta_ref[4 * k + n] for n in range(4)]
            tile = out_ref[dest, per:]
            for n, value in enumerate(values):
                value = jnp.full((per, width), value, jnp.int32).astype(jnp.float32)
                tile = jnp.where(lanes == META_LANE + n, value, tile)
            out_ref[dest, per:] = tile


def local(queries, kv_cache, slot_meta, row_len, new_slot, master):
    slots = kv_cache.shape[0]
    pairs = slots // 2
    rows, heads, width = queries.shape
    per = rows * heads // pairs
    me = lax.axis_index("inst")
    smem = pl.BlockSpec(memory_space=pltpu.SMEM)
    anywhere = pl.BlockSpec(memory_space=pl.ANY)

    outgoing = pl.pallas_call(
        functools.partial(gather_pairs, pairs, slots),
        out_shape=jax.ShapeDtypeStruct(kv_cache.shape, kv_cache.dtype),
        in_specs=[smem, anywhere],
        out_specs=anywhere,
        scratch_shapes=[pltpu.SemaphoreType.DMA((pairs,))],
        name="gather_pairs",
    )(new_slot, kv_cache)
    arrived = lax.all_to_all(outgoing, "inst", split_axis=0, concat_axis=0, tiled=True)

    group = 4
    parts = pl.pallas_call(
        functools.partial(attend_kernel, slots, group),
        out_shape=jax.ShapeDtypeStruct((pairs, 2 * per, width), jnp.float32),
        grid_spec=pltpu.PrefetchScalarGridSpec(
            num_scalar_prefetch=3,
            grid=(slots // group,),
            in_specs=[
                pl.BlockSpec((rows, heads, width), lambda i, *_: (0, 0, 0)),
                pl.BlockSpec((group,) + kv_cache.shape[1:], lambda i, *_: (i, 0, 0, 0, 0)),
            ],
            out_specs=pl.BlockSpec((pairs, 2 * per, width), lambda i, *_: (0, 0, 0)),
            scratch_shapes=[pltpu.VMEM((slots, heads, width), jnp.float32)] * 3,
        ),
        compiler_params=pltpu.CompilerParams(
            dimension_semantics=("arbitrary",), vmem_limit_bytes=16 * 1024 * 1024
        ),
        cost_estimate=pl.CostEstimate(
            flops=6 * slots * heads * kv_cache.shape[3] * width,
            bytes_accessed=kv_cache.size * 2,
            transcendentals=slots * heads * kv_cache.shape[3],
        ),
        name="attend",
    )(slot_meta.reshape(-1), row_len, new_slot, queries, kv_cache)
    mine = lax.all_to_all(parts, "inst", split_axis=0, concat_axis=0, tiled=True)

    details = mine[:, per, META_LANE : META_LANE + 5].astype(jnp.int32)
    place = details[:, 0]
    placing = place[None, :] == jnp.arange(pairs, dtype=jnp.int32)[:, None]
    moved_meta = jnp.sum(
        jnp.where(placing[:, :, None], details[None, :, 1:], 0), axis=1
    ).reshape(slots, 2)

    peaks = mine[:, per:, MAX_LANE : MAX_LANE + 1]
    totals = mine[:, per:, TOTAL_LANE : TOTAL_LANE + 1]
    scale = jnp.exp(peaks - peaks.max(0, keepdims=True))
    done = jnp.sum(mine[:, :per] * scale, axis=0) / jnp.sum(totals * scale, axis=0)
    result = lax.all_gather(done, "inst", axis=0, tiled=True).reshape(1, rows, heads, width)
    attended = jnp.where((master == me)[None, :, None, None], result, jnp.float32(0.0))

    moved_cache = pl.pallas_call(
        functools.partial(place_pairs, pairs),
        out_shape=jax.ShapeDtypeStruct(kv_cache.shape, kv_cache.dtype),
        in_specs=[smem, anywhere],
        out_specs=anywhere,
        scratch_shapes=[pltpu.SemaphoreType.DMA((pairs,))],
        name="place_pairs",
    )(place, arrived)
    return (moved_cache, moved_meta, attended)


def solution(mesh):
    in_specs = (
        P(None, "tp", None),
        P("inst", None, "tp", None, None),
        P("inst", None),
        P(),
        P("inst"),
        P(),
    )
    out_specs = (P("inst", None, "tp", None, None), P("inst", None), P("inst", None, "tp", None))
    return jax.shard_map(local, mesh=mesh, in_specs=in_specs, out_specs=out_specs, check_vma=False)
```

```python
import functools
import math

import jax
import jax.numpy as jnp
from jax import lax
from jax.experimental import pallas as pl
from jax.experimental.pallas import tpu as pltpu
from jax.sharding import PartitionSpec as P

LOWEST = -1e30
BRIEF = pl.CostEstimate(flops=1, bytes_accessed=1, transcendentals=0)
MAX_LANE, TOTAL_LANE, META_LANE = 0, 32, 64


def coordinates(inst, side):
    crossed = lax.axis_index("tp") % 2 == 1
    x, y = inst % side, inst // side
    return jnp.where(crossed, y, x), jnp.where(crossed, x, y)


def instance(first, second, side):
    crossed = lax.axis_index("tp") % 2 == 1
    return jnp.where(crossed, first * side + second, second * side + first)


def by_distance(side, slots, new_slot_ref, order):
    here = coordinates(lax.axis_index("inst"), side)
    for k in range(side * side):
        there = coordinates(new_slot_ref[2 * k] // slots, side)
        first, second = (lax.rem(t - h + side, side) for t, h in zip(there, here))
        order[first * side + second] = k


def gather_plan(hops, side, slots, new_slot_ref, order, in_refs, out_refs):
    by_distance(side, slots, new_slot_ref, order)
    return [
        ((in_refs[0], order[first * side + second]), (out_refs[n], second))
        for n, first in enumerate(hops)
        for second in range(side)
    ]


def stage_plan(turns, side, slots, new_slot_ref, order, in_refs, out_refs):
    by_distance(side, slots, new_slot_ref, order)
    return [
        ((ref, turn if n else order[turn]), (out, n))
        for out, turn in zip(out_refs, turns)
        for n, ref in enumerate(in_refs)
    ]


def split_plan(turns, in_refs, out_refs):
    return [((ref, turn), (out, n)) for out, turn in zip(out_refs, turns) for n, ref in enumerate(in_refs)]


def place_plan(pieces, side, where_ref, in_refs, out_refs):
    first_here, second_here = coordinates(lax.axis_index("inst"), side)
    plan = []
    for source, pair, first, second in pieces:
        origin = instance(
            lax.rem(first_here - first + side, side), lax.rem(second_here - second + side, side), side
        )
        target = where_ref[origin]
        plan.append(((in_refs[source], target if pair is None else pair), (out_refs[0], target)))
    return plan


def move_kernel(plan, n_scalars, n_in, n_out, *refs):
    scalars, in_refs = refs[:n_scalars], refs[n_scalars : n_scalars + n_in]
    out_refs, scratch = refs[n_scalars + n_in :][:n_out], refs[n_scalars + n_in + n_out :]
    buffer, in_sems, out_sems = scratch[-3:]
    loads, stores = [], []
    for n, ((source, m), (target, k)) in enumerate(plan(*scalars, *scratch[:-3], in_refs, out_refs)):
        loads.append(pltpu.make_async_copy(source.at[pl.ds(2 * m, 2)], buffer.at[n], in_sems.at[n]))
        stores.append(pltpu.make_async_copy(buffer.at[n], target.at[pl.ds(2 * k, 2)], out_sems.at[n]))
        loads[-1].start()
    for load, store in zip(loads, stores):
        load.wait()
        store.start()
    for store in stores:
        store.wait()


def move(plan, count, scalars, arrays, out_pairs, name, into=None, scratch=()):
    slot = arrays[0].shape[1:]
    operands = arrays + ([] if into is None else [into])
    smem, anywhere = pl.BlockSpec(memory_space=pltpu.SMEM), pl.BlockSpec(memory_space=pl.ANY)
    size = count * 2 * math.prod(slot) * arrays[0].dtype.itemsize
    return pl.pallas_call(
        functools.partial(move_kernel, plan, len(scalars), len(operands), len(out_pairs)),
        out_shape=[pltpu.HBM((2 * n,) + slot, arrays[0].dtype) for n in out_pairs],
        in_specs=[smem] * len(scalars) + [anywhere] * len(operands),
        out_specs=[anywhere] * len(out_pairs),
        scratch_shapes=list(scratch)
        + [pltpu.VMEM((count, 2) + slot, arrays[0].dtype)]
        + [pltpu.SemaphoreType.DMA((count,))] * 2,
        input_output_aliases={} if into is None else {len(scalars) + len(operands) - 1: 0},
        compiler_params=pltpu.CompilerParams(vmem_limit_bytes=size + 1024 * 1024),
        cost_estimate=BRIEF,
        name=name,
    )(*scalars, *operands)


def shifted(value, side, distance, direction):
    tp = lax.axis_size("tp")
    pairs = []
    for inst in range(side * side):
        for part in range(tp):
            x, y = inst % side, inst // side
            if (part % 2) ^ direction:
                y = (y + distance) % side
            else:
                x = (x + distance) % side
            pairs.append((inst * tp + part, (y * side + x) * tp + part))
    return lax.ppermute(value, ("inst", "tp"), pairs)


def attend_kernel(
    slots, group, meta_ref, len_ref, new_slot_ref, q_ref, kv_ref, out_ref, max_ref, total_ref, sum_ref
):
    step = pl.program_id(0)
    rows, heads, width = q_ref.shape
    block = kv_ref.shape[3]
    lane = lax.broadcasted_iota(jnp.int32, (heads, block), 1)
    for j in range(group):
        slot = step * group + j
        row = meta_ref[2 * slot]
        left = len_ref[row] - meta_ref[2 * slot + 1] * block
        scores = lax.dot_general(
            q_ref[row], kv_ref[j, 0, 0], (((1,), (1,)), ((), ())), preferred_element_type=jnp.float32
        ) * width ** (-0.5)
        valid = lane < left
        scores = jnp.where(valid, scores, LOWEST)
        peak = scores.max(-1, keepdims=True)
        weight = jnp.where(valid, jnp.exp(scores - peak), 0.0)
        high = weight.astype(jnp.bfloat16)
        low = (weight - high.astype(jnp.float32)).astype(jnp.bfloat16)
        both = jnp.dot(
            jnp.concatenate([high, low], axis=0), kv_ref[j, 1, 0], preferred_element_type=jnp.float32
        )
        sum_ref[slot] = both[:heads] + both[heads:]
        max_ref[slot] = jnp.broadcast_to(peak, (heads, width))
        total_ref[slot] = jnp.broadcast_to(weight.sum(-1, keepdims=True), (heads, width))

    @pl.when(step == slots // group - 1)
    def _():
        lanes = lax.broadcasted_iota(jnp.int32, (heads, width), 1)
        per = out_ref.shape[1] // 2
        for row in range(rows):
            peak = jnp.full((heads, width), LOWEST, jnp.float32)
            for slot in range(slots):
                peak = jnp.maximum(peak, jnp.where(meta_ref[2 * slot] == row, max_ref[slot], LOWEST))
            total = jnp.zeros((heads, width), jnp.float32)
            summed = jnp.zeros((heads, width), jnp.float32)
            for slot in range(slots):
                scale = jnp.where(meta_ref[2 * slot] == row, jnp.exp(max_ref[slot] - peak), 0.0)
                total = total + scale * total_ref[slot]
                summed = summed + scale * sum_ref[slot]
            stats = jnp.where(lanes < TOTAL_LANE, peak, total)
            for part in range(heads // per):
                dest = row * (heads // per) + part
                out_ref[dest, :per] = summed[part * per : (part + 1) * per]
                out_ref[dest, per:] = stats[part * per : (part + 1) * per]
        lanes = lax.broadcasted_iota(jnp.int32, (per, width), 1)
        for k in range(slots // 2):
            dest = new_slot_ref[2 * k] // slots
            values = [k] + [meta_ref[4 * k + n] for n in range(4)]
            tile = out_ref[dest, per:]
            for n, value in enumerate(values):
                value = jnp.full((per, width), value, jnp.int32).astype(jnp.float32)
                tile = jnp.where(lanes == META_LANE + n, value, tile)
            out_ref[dest, per:] = tile


def local(queries, kv_cache, slot_meta, row_len, new_slot, master):
    slots = kv_cache.shape[0]
    pairs = slots // 2
    side = math.isqrt(pairs)
    rows, heads, width = queries.shape
    per = rows * heads // pairs
    me = lax.axis_index("inst")

    kv_cache, new_slot = (pltpu.with_memory_space_constraint(array, pltpu.HBM) for array in (kv_cache, new_slot))
    order = pltpu.SMEM((pairs,), jnp.int32)

    def gathered(*hops):
        plan = functools.partial(gather_plan, hops, side, slots)
        return move(
            plan, len(hops) * side, [new_slot], [kv_cache], [side] * len(hops), "gather", scratch=[order]
        )

    def placed(arrays, pieces, into=None):
        plan = functools.partial(place_plan, pieces, side)
        return move(plan, len(pieces), [where], arrays, [pairs], "place", into=into)[0]

    turns = (2, 1, 3)
    (out_two,) = gathered(2)
    got_two = shifted(out_two, side, 2, 0)
    out_one, out_three = gathered(1, 3)
    got_one = shifted(out_one, side, 1, 0)
    got_three = shifted(out_three, side, 3, 0)
    queries, got_two = lax.optimization_barrier((queries, got_two))

    group = 4
    parts = pl.pallas_call(
        functools.partial(attend_kernel, slots, group),
        out_shape=jax.ShapeDtypeStruct((pairs, 2 * per, width), jnp.float32),
        grid_spec=pltpu.PrefetchScalarGridSpec(
            num_scalar_prefetch=3,
            grid=(slots // group,),
            in_specs=[
                pl.BlockSpec((rows, heads, width), lambda i, *_: (0, 0, 0)),
                pl.BlockSpec((group,) + kv_cache.shape[1:], lambda i, *_: (i, 0, 0, 0, 0)),
            ],
            out_specs=pl.BlockSpec((pairs, 2 * per, width), lambda i, *_: (0, 0, 0)),
            scratch_shapes=[pltpu.VMEM((slots, heads, width), jnp.float32)] * 3,
        ),
        compiler_params=pltpu.CompilerParams(
            dimension_semantics=("arbitrary",), vmem_limit_bytes=8 * 1024 * 1024
        ),
        cost_estimate=BRIEF,
        name="attend",
    )(slot_meta.reshape(-1), row_len, new_slot, queries, kv_cache)
    got_two, parts = lax.optimization_barrier((got_two, parts))
    plan = functools.partial(stage_plan, turns, side, slots)
    out_early = move(plan, 6, [new_slot], [kv_cache, got_two], [2] * 3, "stage", scratch=[order])
    got_early = [shifted(array, side, turn, 1) for array, turn in zip(out_early, turns)]
    mine = lax.all_to_all(parts, "inst", split_axis=0, concat_axis=0, tiled=True)
    out_late = move(functools.partial(split_plan, turns), 6, [], [got_one, got_three], [2] * 3, "split")
    got_late = [shifted(out_late[0], side, 2, 1)]
    out_late, got_early = lax.optimization_barrier((out_late, got_early))
    got_late += [shifted(array, side, turn, 1) for array, turn in zip(out_late[1:], turns[1:])]

    details = mine[:, per, META_LANE : META_LANE + 5].astype(jnp.int32)
    where = details[:, 0]
    placing = where[None, :] == jnp.arange(pairs, dtype=jnp.int32)[:, None]
    moved_meta = jnp.sum(
        jnp.where(placing[:, :, None], details[None, :, 1:], 0), axis=1
    ).reshape(slots, 2)
    pieces = [(0, None, 0, 0), (1, 0, 2, 0), (2, 0, 1, 0), (3, 0, 3, 0)]
    pieces += [(4 + n, m, first, turn) for n, turn in enumerate(turns) for m, first in enumerate((0, 2))]
    moved_cache = placed([kv_cache, got_two, got_one, got_three] + got_early, pieces)

    peaks = mine[:, per:, MAX_LANE : MAX_LANE + 1]
    totals = mine[:, per:, TOTAL_LANE : TOTAL_LANE + 1]
    scale = jnp.exp(peaks - peaks.max(0, keepdims=True))
    done = jnp.sum(mine[:, :per] * scale, axis=0) / jnp.sum(totals * scale, axis=0)
    done, moved_cache = lax.optimization_barrier((done, moved_cache))
    everyone = jnp.broadcast_to(done[None], (pairs,) + done.shape)
    result = lax.all_to_all(everyone, "inst", split_axis=0, concat_axis=0, tiled=True)
    result = result.reshape(1, rows, heads, width)
    attended = jnp.where((master == me)[None, :, None, None], result, jnp.float32(0.0))

    moved_cache = placed(got_late[:1], [(0, m, first, 2) for m, first in enumerate((1, 3))], moved_cache)
    pieces = [(n, m, first, turn) for n, turn in enumerate(turns[1:]) for m, first in enumerate((1, 3))]
    moved_cache = placed(got_late[1:], pieces, moved_cache)
    return (moved_cache, moved_meta, attended)


def solution(mesh):
    in_specs = (
        P(None, "tp", None),
        P("inst", None, "tp", None, None),
        P("inst", None),
        P(),
        P("inst"),
        P(),
    )
    out_specs = (P("inst", None, "tp", None, None), P("inst", None), P("inst", None, "tp", None))
    return jax.shard_map(local, mesh=mesh, in_specs=in_specs, out_specs=out_specs, check_vma=False)
```

```python
import functools
import math

import jax
import jax.numpy as jnp
from jax import lax
from jax.experimental import pallas as pl
from jax.experimental.pallas import tpu as pltpu
from jax.sharding import PartitionSpec as P

LOWEST = -1e30
BRIEF = pl.CostEstimate(flops=1, bytes_accessed=1, transcendentals=0)
MAX_LANE, TOTAL_LANE, META_LANE = 0, 32, 64


def bits(size):
    assert size & (size - 1) == 0
    return size.bit_length() - 1


def coordinates(inst, side):
    crossed = lax.axis_index("tp") % 2 == 1
    x, y = inst & (side - 1), lax.shift_right_logical(inst, bits(side))
    return jnp.where(crossed, y, x), jnp.where(crossed, x, y)


def instance(first, second, side):
    crossed = lax.axis_index("tp") % 2 == 1
    return jnp.where(crossed, first * side + second, second * side + first)


def by_distance(side, slots, new_slot_ref, order):
    here = lax.axis_index("inst")
    x, y = here & (side - 1), lax.shift_right_logical(here, bits(side))
    for k in range(side * side):
        there = lax.shift_right_logical(new_slot_ref[2 * k], bits(slots))
        across = (there - x) & (side - 1)
        order[((lax.shift_right_logical(there, bits(side)) - y) & (side - 1)) * side + across] = k
    return lambda first, second: order[instance(first, second, side)]


def known_already():
    pass


def gather_plan(hops, side, slots, new_slot_ref, in_refs, out_refs, order):
    pair = by_distance(side, slots, new_slot_ref, order)
    pieces = [
        ((in_refs[0], pair(first, second)), (out, second))
        for out, first in zip(out_refs, hops)
        for second in range(side)
    ]
    return pieces, known_already


def stage_plan(turns, side, slots, new_slot_ref, in_refs, out_refs, order):
    pair = by_distance(side, slots, new_slot_ref, order)
    pieces = [
        ((ref, turn if n else pair(0, turn)), (out, n))
        for out, turn in zip(out_refs, turns)
        for n, ref in enumerate(in_refs)
    ]
    return pieces, known_already


def split_plan(turns, in_refs, out_refs):
    pieces = [((ref, turn), (out, n)) for out, turn in zip(out_refs, turns) for n, ref in enumerate(in_refs)]
    return pieces, known_already


def place_plan(pieces, side, where_at, in_refs, out_refs, where, sem):
    first_here, second_here = coordinates(lax.axis_index("inst"), side)
    fetch = pltpu.make_async_copy(in_refs[where_at], where, sem)
    fetch.start()
    plan = []
    for source, pair, first, second in pieces:
        origin = instance(
            (first_here - first) & (side - 1), (second_here - second) & (side - 1), side
        )
        target = functools.partial(where.__getitem__, origin)
        plan.append(((in_refs[source], target if pair is None else pair), (out_refs[0], target)))
    return plan, fetch.wait


def move_kernel(plan, n_scalars, n_in, n_out, *refs):
    scalars, in_refs = refs[:n_scalars], refs[n_scalars : n_scalars + n_in]
    out_refs, scratch = refs[n_scalars + n_in :][:n_out], refs[n_scalars + n_in + n_out :]
    *scratch, buffer, in_sems, out_sems = scratch
    pieces, known = plan(*scalars, in_refs, out_refs, *scratch)

    def part(ref, pair):
        return ref.at[pl.ds(2 * (pair() if callable(pair) else pair), 2)]

    def load(n):
        copy = pltpu.make_async_copy(part(*pieces[n][0]), buffer.at[n], in_sems.at[n])
        copy.start()
        return copy

    loads = [None if callable(pair) else load(n) for n, ((_, pair), _) in enumerate(pieces)]
    known()
    loads = [copy or load(n) for n, copy in enumerate(loads)]
    stores = []
    for n, copy in enumerate(loads):
        copy.wait()
        stores.append(pltpu.make_async_copy(buffer.at[n], part(*pieces[n][1]), out_sems.at[n]))
        stores[-1].start()
    for copy in stores:
        copy.wait()


def move(plan, count, scalars, arrays, out_pairs, name, into=None, scratch=()):
    slot = arrays[0].shape[1:]
    operands = arrays + ([] if into is None else [into])
    smem, anywhere = pl.BlockSpec(memory_space=pltpu.SMEM), pl.BlockSpec(memory_space=pl.ANY)
    size = count * 2 * math.prod(slot) * arrays[0].dtype.itemsize
    return pl.pallas_call(
        functools.partial(move_kernel, plan, len(scalars), len(operands), len(out_pairs)),
        out_shape=[pltpu.HBM((2 * n,) + slot, arrays[0].dtype) for n in out_pairs],
        in_specs=[smem] * len(scalars) + [anywhere] * len(operands),
        out_specs=[anywhere] * len(out_pairs),
        scratch_shapes=list(scratch)
        + [pltpu.VMEM((count, 2) + slot, arrays[0].dtype)]
        + [pltpu.SemaphoreType.DMA((count,))] * 2,
        input_output_aliases={} if into is None else {len(scalars) + len(operands) - 1: 0},
        compiler_params=pltpu.CompilerParams(vmem_limit_bytes=size + 1024 * 1024),
        cost_estimate=BRIEF,
        name=name,
    )(*scalars, *operands)


def shifted(value, side, distance, direction):
    tp = lax.axis_size("tp")
    pairs = []
    for inst in range(side * side):
        for part in range(tp):
            x, y = inst % side, inst // side
            if (part % 2) ^ direction:
                y = (y + distance) % side
            else:
                x = (x + distance) % side
            pairs.append((inst * tp + part, (y * side + x) * tp + part))
    return lax.ppermute(value, ("inst", "tp"), pairs)


def attend_kernel(
    slots, group, meta_ref, len_ref, new_slot_ref, q_ref, kv_ref, out_ref, max_ref, total_ref, sum_ref
):
    step = pl.program_id(0)
    rows, heads, width = q_ref.shape
    block = kv_ref.shape[3]
    lane = lax.broadcasted_iota(jnp.int32, (heads, block), 1)
    for j in range(group):
        slot = step * group + j
        row = meta_ref[2 * slot]
        left = len_ref[row] - meta_ref[2 * slot + 1] * block
        scores = lax.dot_general(
            q_ref[row], kv_ref[j, 0, 0], (((1,), (1,)), ((), ())), preferred_element_type=jnp.float32
        ) * width ** (-0.5)
        valid = lane < left
        scores = jnp.where(valid, scores, LOWEST)
        peak = scores.max(-1, keepdims=True)
        weight = jnp.where(valid, jnp.exp(scores - peak), 0.0)
        high = weight.astype(jnp.bfloat16)
        low = (weight - high.astype(jnp.float32)).astype(jnp.bfloat16)
        both = jnp.dot(
            jnp.concatenate([high, low], axis=0), kv_ref[j, 1, 0], preferred_element_type=jnp.float32
        )
        sum_ref[slot] = both[:heads] + both[heads:]
        max_ref[slot] = jnp.broadcast_to(peak, (heads, width))
        total_ref[slot] = jnp.broadcast_to(weight.sum(-1, keepdims=True), (heads, width))

    @pl.when(step == slots // group - 1)
    def _():
        lanes = lax.broadcasted_iota(jnp.int32, (heads, width), 1)
        per = out_ref.shape[1] // 2
        for row in range(rows):
            peak = jnp.full((heads, width), LOWEST, jnp.float32)
            for slot in range(slots):
                peak = jnp.maximum(peak, jnp.where(meta_ref[2 * slot] == row, max_ref[slot], LOWEST))
            total = jnp.zeros((heads, width), jnp.float32)
            summed = jnp.zeros((heads, width), jnp.float32)
            for slot in range(slots):
                scale = jnp.where(meta_ref[2 * slot] == row, jnp.exp(max_ref[slot] - peak), 0.0)
                total = total + scale * total_ref[slot]
                summed = summed + scale * sum_ref[slot]
            stats = jnp.where(lanes < TOTAL_LANE, peak, total)
            for part in range(heads // per):
                dest = row * (heads // per) + part
                out_ref[dest, :per] = summed[part * per : (part + 1) * per]
                out_ref[dest, per:] = stats[part * per : (part + 1) * per]
        lanes = lax.broadcasted_iota(jnp.int32, (per, width), 1)
        for k in range(slots // 2):
            dest = new_slot_ref[2 * k] // slots
            values = [k] + [meta_ref[4 * k + n] for n in range(4)]
            tile = out_ref[dest, per:]
            for n, value in enumerate(values):
                value = jnp.full((per, width), value, jnp.int32).astype(jnp.float32)
                tile = jnp.where(lanes == META_LANE + n, value, tile)
            out_ref[dest, per:] = tile


def local(queries, kv_cache, slot_meta, row_len, new_slot, master):
    slots = kv_cache.shape[0]
    pairs = slots // 2
    side = math.isqrt(pairs)
    rows, heads, width = queries.shape
    per = rows * heads // pairs
    me = lax.axis_index("inst")

    kv_cache, new_slot = (pltpu.with_memory_space_constraint(array, pltpu.HBM) for array in (kv_cache, new_slot))
    order = pltpu.SMEM((pairs,), jnp.int32)

    def gathered(*hops):
        plan = functools.partial(gather_plan, hops, side, slots)
        return move(
            plan, len(hops) * side, [new_slot], [kv_cache], [side] * len(hops), "gather", scratch=[order]
        )

    def placed(arrays, pieces, into=None):
        plan = functools.partial(place_plan, pieces, side, len(arrays))
        scratch = [order, pltpu.SemaphoreType.DMA]
        return move(plan, len(pieces), [], arrays + [where], [pairs], "place", into=into, scratch=scratch)[0]

    turns = (2, 1, 3)
    (out_two,) = gathered(2)
    got_two = shifted(out_two, side, 2, 0)
    out_one, out_three = gathered(1, 3)
    got_one = shifted(out_one, side, 1, 0)
    got_three = shifted(out_three, side, 3, 0)
    queries, got_two = lax.optimization_barrier((queries, got_two))

    group = 4
    parts = pl.pallas_call(
        functools.partial(attend_kernel, slots, group),
        out_shape=jax.ShapeDtypeStruct((pairs, 2 * per, width), jnp.float32),
        grid_spec=pltpu.PrefetchScalarGridSpec(
            num_scalar_prefetch=3,
            grid=(slots // group,),
            in_specs=[
                pl.BlockSpec((rows, heads, width), lambda i, *_: (0, 0, 0)),
                pl.BlockSpec((group,) + kv_cache.shape[1:], lambda i, *_: (i, 0, 0, 0, 0)),
            ],
            out_specs=pl.BlockSpec((pairs, 2 * per, width), lambda i, *_: (0, 0, 0)),
            scratch_shapes=[pltpu.VMEM((slots, heads, width), jnp.float32)] * 3,
        ),
        compiler_params=pltpu.CompilerParams(
            dimension_semantics=("arbitrary",), vmem_limit_bytes=8 * 1024 * 1024
        ),
        cost_estimate=BRIEF,
        name="attend",
    )(slot_meta.reshape(-1), row_len, new_slot, queries, kv_cache)
    got_two, parts = lax.optimization_barrier((got_two, parts))
    plan = functools.partial(stage_plan, turns, side, slots)
    out_early = move(plan, 6, [new_slot], [kv_cache, got_two], [2] * 3, "stage", scratch=[order])
    got_early = [shifted(array, side, turn, 1) for array, turn in zip(out_early, turns)]
    mine = lax.all_to_all(parts, "inst", split_axis=0, concat_axis=0, tiled=True)
    out_late = move(functools.partial(split_plan, turns), 6, [], [got_one, got_three], [2] * 3, "split")
    got_late = [shifted(out_late[0], side, 2, 1)]
    out_late, got_early = lax.optimization_barrier((out_late, got_early))
    got_late += [shifted(array, side, turn, 1) for array, turn in zip(out_late[1:], turns[1:])]

    details = mine[:, per, META_LANE : META_LANE + 5].astype(jnp.int32)
    where = details[:, 0]
    placing = where[None, :] == jnp.arange(pairs, dtype=jnp.int32)[:, None]
    moved_meta = jnp.sum(
        jnp.where(placing[:, :, None], details[None, :, 1:], 0), axis=1
    ).reshape(slots, 2)
    pieces = [(0, None, 0, 0), (1, 0, 2, 0), (2, 0, 1, 0), (3, 0, 3, 0)]
    pieces += [(4 + n, m, first, turn) for n, turn in enumerate(turns) for m, first in enumerate((0, 2))]
    moved_cache = placed([kv_cache, got_two, got_one, got_three] + got_early, pieces)

    peaks = mine[:, per:, MAX_LANE : MAX_LANE + 1]
    totals = mine[:, per:, TOTAL_LANE : TOTAL_LANE + 1]
    scale = jnp.exp(peaks - peaks.max(0, keepdims=True))
    done = jnp.sum(mine[:, :per] * scale, axis=0) / jnp.sum(totals * scale, axis=0)
    everyone = jnp.broadcast_to(done[None], (pairs,) + done.shape)
    result = lax.all_to_all(everyone, "inst", split_axis=0, concat_axis=0, tiled=True)
    result = result.reshape(1, rows, heads, width)
    moved_cache = placed(got_late[:1], [(0, m, first, 2) for m, first in enumerate((1, 3))], moved_cache)
    pieces = [(n, m, first, turn) for n, turn in enumerate(turns[1:]) for m, first in enumerate((1, 3))]
    moved_cache = placed(got_late[1:], pieces, moved_cache)
    result, moved_cache = lax.optimization_barrier((result, moved_cache))
    attended = jnp.where((master == me)[None, :, None, None], result, jnp.float32(0.0))
    return (moved_cache, moved_meta, attended)


def solution(mesh):
    in_specs = (
        P(None, "tp", None),
        P("inst", None, "tp", None, None),
        P("inst", None),
        P(),
        P("inst"),
        P(),
    )
    out_specs = (P("inst", None, "tp", None, None), P("inst", None), P("inst", None, "tp", None))
    return jax.shard_map(local, mesh=mesh, in_specs=in_specs, out_specs=out_specs, check_vma=False)
```

```python
import functools
import math

import jax
import jax.numpy as jnp
from jax import lax
from jax.experimental import pallas as pl
from jax.experimental.pallas import tpu as pltpu
from jax.sharding import PartitionSpec as P

LOWEST = -1e30
BRIEF = pl.CostEstimate(flops=1, bytes_accessed=1, transcendentals=0)
MAX_LANE, TOTAL_LANE, META_LANE = 0, 32, 64


def bits(size):
    assert size & (size - 1) == 0
    return size.bit_length() - 1


def coordinates(inst, side):
    crossed = lax.axis_index("tp") % 2 == 1
    x, y = inst & (side - 1), lax.shift_right_logical(inst, bits(side))
    return jnp.where(crossed, y, x), jnp.where(crossed, x, y)


def instance(first, second, side):
    crossed = lax.axis_index("tp") % 2 == 1
    return jnp.where(crossed, first * side + second, second * side + first)


def by_distance(side, slots, new_slot_ref, order):
    here = lax.axis_index("inst")
    x, y = here & (side - 1), lax.shift_right_logical(here, bits(side))
    for k in range(side * side):
        there = lax.shift_right_logical(new_slot_ref[2 * k], bits(slots))
        across = (there - x) & (side - 1)
        order[((lax.shift_right_logical(there, bits(side)) - y) & (side - 1)) * side + across] = k
    return lambda first, second: order[instance(first, second, side)]


def known_already():
    pass


def gather_plan(hops, side, slots, new_slot_ref, in_refs, out_refs, order):
    pair = by_distance(side, slots, new_slot_ref, order)
    pieces = [
        ((in_refs[0], pair(first, second)), (out, second))
        for out, first in zip(out_refs, hops)
        for second in range(side)
    ]
    return pieces, known_already


def stage_plan(turns, side, slots, new_slot_ref, in_refs, out_refs, order):
    pair = by_distance(side, slots, new_slot_ref, order)
    pieces = [
        ((ref, turn if n else pair(0, turn)), (out, n))
        for out, turn in zip(out_refs, turns)
        for n, ref in enumerate(in_refs)
    ]
    return pieces, known_already


def split_plan(parts, in_refs, out_refs):
    pieces = [
        ((in_refs[ref], turn), (out, n)) for out, (turn, refs) in zip(out_refs, parts) for n, ref in enumerate(refs)
    ]
    return pieces, known_already


def place_plan(pieces, side, where_at, in_refs, out_refs, where, sem):
    first_here, second_here = coordinates(lax.axis_index("inst"), side)
    fetch = pltpu.make_async_copy(in_refs[where_at], where, sem)
    fetch.start()
    plan = []
    for source, pair, first, second in pieces:
        origin = instance(
            (first_here - first) & (side - 1), (second_here - second) & (side - 1), side
        )
        target = functools.partial(where.__getitem__, origin)
        plan.append(((in_refs[source], target if pair is None else pair), (out_refs[0], target)))
    return plan, fetch.wait


def move_kernel(plan, n_scalars, n_in, n_out, *refs):
    scalars, in_refs = refs[:n_scalars], refs[n_scalars : n_scalars + n_in]
    out_refs, scratch = refs[n_scalars + n_in :][:n_out], refs[n_scalars + n_in + n_out :]
    *scratch, buffer, in_sems, out_sems = scratch
    pieces, known = plan(*scalars, in_refs, out_refs, *scratch)

    def part(ref, pair):
        return ref.at[pl.ds(2 * (pair() if callable(pair) else pair), 2)]

    def load(n):
        copy = pltpu.make_async_copy(part(*pieces[n][0]), buffer.at[n], in_sems.at[n])
        copy.start()
        return copy

    loads = [None if callable(pair) else load(n) for n, ((_, pair), _) in enumerate(pieces)]
    known()
    loads = [copy or load(n) for n, copy in enumerate(loads)]
    stores = []
    for n, copy in enumerate(loads):
        copy.wait()
        stores.append(pltpu.make_async_copy(buffer.at[n], part(*pieces[n][1]), out_sems.at[n]))
        stores[-1].start()
    for copy in stores:
        copy.wait()


def move(plan, count, scalars, arrays, out_pairs, name, into=None, scratch=()):
    slot = arrays[0].shape[1:]
    operands = arrays + ([] if into is None else [into])
    smem, anywhere = pl.BlockSpec(memory_space=pltpu.SMEM), pl.BlockSpec(memory_space=pl.ANY)
    size = count * 2 * math.prod(slot) * arrays[0].dtype.itemsize
    return pl.pallas_call(
        functools.partial(move_kernel, plan, len(scalars), len(operands), len(out_pairs)),
        out_shape=[pltpu.HBM((2 * n,) + slot, arrays[0].dtype) for n in out_pairs],
        in_specs=[smem] * len(scalars) + [anywhere] * len(operands),
        out_specs=[anywhere] * len(out_pairs),
        scratch_shapes=list(scratch)
        + [pltpu.VMEM((count, 2) + slot, arrays[0].dtype)]
        + [pltpu.SemaphoreType.DMA((count,))] * 2,
        input_output_aliases={} if into is None else {len(scalars) + len(operands) - 1: 0},
        compiler_params=pltpu.CompilerParams(vmem_limit_bytes=size + 1024 * 1024),
        cost_estimate=BRIEF,
        name=name,
    )(*scalars, *operands)


def shifted(value, side, distance, direction):
    tp = lax.axis_size("tp")
    pairs = []
    for inst in range(side * side):
        for part in range(tp):
            x, y = inst % side, inst // side
            if (part % 2) ^ direction:
                y = (y + distance) % side
            else:
                x = (x + distance) % side
            pairs.append((inst * tp + part, (y * side + x) * tp + part))
    return lax.ppermute(value, ("inst", "tp"), pairs)


def attend_slots(start, group, meta_ref, len_ref, q_ref, kv_ref, max_ref, total_ref, sum_ref):
    step = pl.program_id(0)
    heads, width = q_ref.shape[1:]
    block = kv_ref.shape[3]
    lane = lax.broadcasted_iota(jnp.int32, (heads, block), 1)
    for j in range(group):
        at = step * group + j
        slot = start + at
        row = meta_ref[2 * slot]
        left = len_ref[row] - meta_ref[2 * slot + 1] * block
        scores = lax.dot_general(
            q_ref[row], kv_ref[j, 0, 0], (((1,), (1,)), ((), ())), preferred_element_type=jnp.float32
        ) * width ** (-0.5)
        valid = lane < left
        scores = jnp.where(valid, scores, LOWEST)
        peak = scores.max(-1, keepdims=True)
        weight = jnp.where(valid, jnp.exp(scores - peak), 0.0)
        high = weight.astype(jnp.bfloat16)
        low = (weight - high.astype(jnp.float32)).astype(jnp.bfloat16)
        both = jnp.dot(
            jnp.concatenate([high, low], axis=0), kv_ref[j, 1, 0], preferred_element_type=jnp.float32
        )
        sum_ref[at] = both[:heads] + both[heads:]
        max_ref[at] = jnp.broadcast_to(peak, (heads, width))
        total_ref[at] = jnp.broadcast_to(weight.sum(-1, keepdims=True), (heads, width))


def attend_early(group, meta_ref, len_ref, q_ref, kv_ref, max_ref, total_ref, sum_ref):
    attend_slots(0, group, meta_ref, len_ref, q_ref, kv_ref, max_ref, total_ref, sum_ref)


def attend_late(slots, start, group, meta_ref, len_ref, new_slot_ref, q_ref, kv_ref, *refs):
    early, out_ref, late = refs[:3], refs[3], refs[4:]
    attend_slots(start, group, meta_ref, len_ref, q_ref, kv_ref, *late)

    @pl.when(pl.program_id(0) == (slots - start) // group - 1)
    def _():
        rows, heads, width = q_ref.shape
        lanes = lax.broadcasted_iota(jnp.int32, (heads, width), 1)
        per = out_ref.shape[1] // 2

        def of_slot(slot):
            return [ref[slot] for ref in early] if slot < start else [ref[slot - start] for ref in late]

        for row in range(rows):
            peak = jnp.full((heads, width), LOWEST, jnp.float32)
            for slot in range(slots):
                peak = jnp.maximum(peak, jnp.where(meta_ref[2 * slot] == row, of_slot(slot)[0], LOWEST))
            total = jnp.zeros((heads, width), jnp.float32)
            summed = jnp.zeros((heads, width), jnp.float32)
            for slot in range(slots):
                slot_max, slot_total, slot_sum = of_slot(slot)
                scale = jnp.where(meta_ref[2 * slot] == row, jnp.exp(slot_max - peak), 0.0)
                total = total + scale * slot_total
                summed = summed + scale * slot_sum
            stats = jnp.where(lanes < TOTAL_LANE, peak, total)
            for part in range(heads // per):
                dest = row * (heads // per) + part
                out_ref[dest, :per] = summed[part * per : (part + 1) * per]
                out_ref[dest, per:] = stats[part * per : (part + 1) * per]
        lanes = lax.broadcasted_iota(jnp.int32, (per, width), 1)
        for k in range(slots // 2):
            dest = new_slot_ref[2 * k] // slots
            values = [k] + [meta_ref[4 * k + n] for n in range(4)]
            tile = out_ref[dest, per:]
            for n, value in enumerate(values):
                value = jnp.full((per, width), value, jnp.int32).astype(jnp.float32)
                tile = jnp.where(lanes == META_LANE + n, value, tile)
            out_ref[dest, per:] = tile


def local(queries, kv_cache, slot_meta, row_len, new_slot, master):
    slots = kv_cache.shape[0]
    pairs = slots // 2
    side = math.isqrt(pairs)
    rows, heads, width = queries.shape
    per = rows * heads // pairs
    me = lax.axis_index("inst")

    kv_cache, new_slot = (pltpu.with_memory_space_constraint(array, pltpu.HBM) for array in (kv_cache, new_slot))
    order = pltpu.SMEM((pairs,), jnp.int32)

    def gathered(*hops):
        plan = functools.partial(gather_plan, hops, side, slots)
        return move(
            plan, len(hops) * side, [new_slot], [kv_cache], [side] * len(hops), "gather", scratch=[order]
        )

    def placed(arrays, pieces, into=None):
        plan = functools.partial(place_plan, pieces, side, len(arrays))
        scratch = [order, pltpu.SemaphoreType.DMA]
        return move(plan, len(pieces), [], arrays + [where], [pairs], "place", into=into, scratch=scratch)[0]

    turns = (2, 1, 3)
    (out_two,) = gathered(2)
    got_two = shifted(out_two, side, 2, 0)
    out_one, out_three = gathered(1, 3)
    got_one = shifted(out_one, side, 1, 0)
    got_three = shifted(out_three, side, 3, 0)
    queries, out_one = lax.optimization_barrier((queries, out_one))

    group = 4
    start = 20 // group * group
    whole = pl.BlockSpec((rows, heads, width), lambda i, *_: (0, 0, 0))
    partial = [jax.ShapeDtypeStruct((start, heads, width), jnp.float32)] * 3
    partial_specs = [pl.BlockSpec((start, heads, width), lambda i, *_: (0, 0, 0))] * 3
    params = pltpu.CompilerParams(dimension_semantics=("arbitrary",), vmem_limit_bytes=8 * 1024 * 1024)
    meta = slot_meta.reshape(-1)
    early = pl.pallas_call(
        functools.partial(attend_early, group),
        out_shape=partial,
        grid_spec=pltpu.PrefetchScalarGridSpec(
            num_scalar_prefetch=2,
            grid=(start // group,),
            in_specs=[whole, pl.BlockSpec((group,) + kv_cache.shape[1:], lambda i, *_: (i, 0, 0, 0, 0))],
            out_specs=partial_specs,
        ),
        compiler_params=params,
        cost_estimate=BRIEF,
        name="attend_early",
    )(meta, row_len, queries, kv_cache)
    early, got_two = lax.optimization_barrier((early, got_two))
    parts = pl.pallas_call(
        functools.partial(attend_late, slots, start, group),
        out_shape=jax.ShapeDtypeStruct((pairs, 2 * per, width), jnp.float32),
        grid_spec=pltpu.PrefetchScalarGridSpec(
            num_scalar_prefetch=3,
            grid=((slots - start) // group,),
            in_specs=[
                whole,
                pl.BlockSpec((group,) + kv_cache.shape[1:], lambda i, *_: (i + start // group, 0, 0, 0, 0)),
            ]
            + partial_specs,
            out_specs=pl.BlockSpec((pairs, 2 * per, width), lambda i, *_: (0, 0, 0)),
            scratch_shapes=[pltpu.VMEM((slots - start, heads, width), jnp.float32)] * 3,
        ),
        compiler_params=params,
        cost_estimate=BRIEF,
        name="attend_late",
    )(meta, row_len, new_slot, queries, kv_cache, *early)
    got_two, parts = lax.optimization_barrier((got_two, parts))
    plan = functools.partial(stage_plan, turns, side, slots)
    out_early = move(plan, 6, [new_slot], [kv_cache, got_two], [2] * 3, "stage", scratch=[order])
    got_early = [shifted(array, side, turn, 1) for array, turn in zip(out_early, turns)]
    mine = lax.all_to_all(parts, "inst", split_axis=0, concat_axis=0, tiled=True)
    got_one, got_three, out_early = lax.optimization_barrier((got_one, got_three, out_early))
    plan = functools.partial(split_plan, ((2, (0, 1)), (1, (0,)), (3, (0,)), (1, (1,)), (3, (1,))))
    out_late = move(plan, 6, [], [got_one, got_three], [2, 1, 1, 1, 1], "split")
    got_late = [shifted(out_late[0], side, 2, 1)]
    out_late, got_early = lax.optimization_barrier((out_late, got_early))
    got_late += [shifted(array, side, turn, 1) for array, turn in zip(out_late[1:3], turns[1:])]
    details = mine[:, per, META_LANE : META_LANE + 5].astype(jnp.int32)
    where = details[:, 0]
    placing = where[None, :] == jnp.arange(pairs, dtype=jnp.int32)[:, None]
    moved_meta = jnp.sum(
        jnp.where(placing[:, :, None], details[None, :, 1:], 0), axis=1
    ).reshape(slots, 2)
    pieces = [(0, None, 0, 0), (1, 0, 2, 0), (2, 0, 1, 0), (3, 0, 3, 0)]
    pieces += [(4 + n, m, first, turn) for n, turn in enumerate(turns) for m, first in enumerate((0, 2))]
    moved_cache = placed([kv_cache, got_two, got_one, got_three] + got_early, pieces)

    out_last, got_late[0], moved_cache = lax.optimization_barrier((out_late[3:], got_late[0], moved_cache))
    got_last = [shifted(array, side, turn, 1) for array, turn in zip(out_last, turns[1:])]

    peaks = mine[:, per:, MAX_LANE : MAX_LANE + 1]
    totals = mine[:, per:, TOTAL_LANE : TOTAL_LANE + 1]
    scale = jnp.exp(peaks - peaks.max(0, keepdims=True))
    done = jnp.sum(mine[:, :per] * scale, axis=0) / jnp.sum(totals * scale, axis=0)
    everyone = jnp.broadcast_to(done[None], (pairs,) + done.shape)
    result = lax.all_to_all(everyone, "inst", split_axis=0, concat_axis=0, tiled=True)
    result = result.reshape(1, rows, heads, width)
    pieces = [(0, 0, 1, 2), (0, 1, 3, 2), (1, 0, 1, 1), (2, 0, 1, 3)]
    moved_cache = placed(got_late, pieces, moved_cache)
    attended = jnp.where((master == me)[None, :, None, None], result, jnp.float32(0.0))
    moved_cache = placed(got_last, [(0, 0, 3, 1), (1, 0, 3, 3)], moved_cache)
    return (moved_cache, moved_meta, attended)


def solution(mesh):
    in_specs = (
        P(None, "tp", None),
        P("inst", None, "tp", None, None),
        P("inst", None),
        P(),
        P("inst"),
        P(),
    )
    out_specs = (P("inst", None, "tp", None, None), P("inst", None), P("inst", None, "tp", None))
    return jax.shard_map(local, mesh=mesh, in_specs=in_specs, out_specs=out_specs, check_vma=False)
```

```python
import functools
import math

import jax
import jax.numpy as jnp
from jax import lax
from jax.experimental import pallas as pl
from jax.experimental.pallas import tpu as pltpu
from jax.sharding import PartitionSpec as P

LOWEST = -1e30
BRIEF = pl.CostEstimate(flops=1, bytes_accessed=1, transcendentals=0)
MAX_LANE, TOTAL_LANE, META_LANE = 0, 32, 64


def bits(size):
    assert size & (size - 1) == 0
    return size.bit_length() - 1


def coordinates(inst, side):
    crossed = lax.axis_index("tp") % 2 == 1
    x, y = inst & (side - 1), lax.shift_right_logical(inst, bits(side))
    return jnp.where(crossed, y, x), jnp.where(crossed, x, y)


def instance(first, second, side):
    crossed = lax.axis_index("tp") % 2 == 1
    return jnp.where(crossed, first * side + second, second * side + first)


def by_distance(side, slots, new_slot_ref, order):
    here = lax.axis_index("inst")
    x, y = here & (side - 1), lax.shift_right_logical(here, bits(side))
    for k in range(side * side):
        there = lax.shift_right_logical(new_slot_ref[2 * k], bits(slots))
        across = (there - x) & (side - 1)
        order[((lax.shift_right_logical(there, bits(side)) - y) & (side - 1)) * side + across] = k
    return lambda first, second: order[instance(first, second, side)]


def known_already():
    pass


def gather_plan(hops, side, slots, new_slot_ref, in_refs, out_refs, order):
    pair = by_distance(side, slots, new_slot_ref, order)
    pieces = [
        ((in_refs[0], pair(first, second)), (out, second))
        for out, first in zip(out_refs, hops)
        for second in range(side)
    ]
    return pieces, known_already


def stage_plan(turns, side, slots, new_slot_ref, in_refs, out_refs, order):
    pair = by_distance(side, slots, new_slot_ref, order)
    pieces = [
        ((ref, turn if n else pair(0, turn)), (out, n))
        for out, turn in zip(out_refs, turns)
        for n, ref in enumerate(in_refs)
    ]
    return pieces, known_already


def split_plan(parts, in_refs, out_refs):
    pieces = [
        ((in_refs[ref], turn), (out, n)) for out, (turn, refs) in zip(out_refs, parts) for n, ref in enumerate(refs)
    ]
    return pieces, known_already


def place_plan(pieces, side, where_at, in_refs, out_refs, where, sem):
    first_here, second_here = coordinates(lax.axis_index("inst"), side)
    fetch = pltpu.make_async_copy(in_refs[where_at], where, sem)
    fetch.start()
    plan = []
    for source, pair, first, second in pieces:
        origin = instance(
            (first_here - first) & (side - 1), (second_here - second) & (side - 1), side
        )
        target = functools.partial(where.__getitem__, origin)
        plan.append(((in_refs[source], target if pair is None else pair), (out_refs[0], target)))
    return plan, fetch.wait


def move_kernel(plan, n_scalars, n_in, n_out, *refs):
    scalars, in_refs = refs[:n_scalars], refs[n_scalars : n_scalars + n_in]
    out_refs, scratch = refs[n_scalars + n_in :][:n_out], refs[n_scalars + n_in + n_out :]
    *scratch, buffer, in_sems, out_sems = scratch
    pieces, known = plan(*scalars, in_refs, out_refs, *scratch)

    def part(ref, pair):
        return ref.at[pl.ds(2 * (pair() if callable(pair) else pair), 2)]

    def load(n):
        copy = pltpu.make_async_copy(part(*pieces[n][0]), buffer.at[n], in_sems.at[n])
        copy.start()
        return copy

    loads = [None if callable(pair) else load(n) for n, ((_, pair), _) in enumerate(pieces)]
    known()
    loads = [copy or load(n) for n, copy in enumerate(loads)]
    stores = []
    for n, copy in enumerate(loads):
        copy.wait()
        stores.append(pltpu.make_async_copy(buffer.at[n], part(*pieces[n][1]), out_sems.at[n]))
        stores[-1].start()
    for copy in stores:
        copy.wait()


def move(plan, count, scalars, arrays, out_pairs, name, into=None, scratch=()):
    slot = arrays[0].shape[1:]
    operands = arrays + ([] if into is None else [into])
    smem, anywhere = pl.BlockSpec(memory_space=pltpu.SMEM), pl.BlockSpec(memory_space=pl.ANY)
    size = count * 2 * math.prod(slot) * arrays[0].dtype.itemsize
    return pl.pallas_call(
        functools.partial(move_kernel, plan, len(scalars), len(operands), len(out_pairs)),
        out_shape=[pltpu.HBM((2 * n,) + slot, arrays[0].dtype) for n in out_pairs],
        in_specs=[smem] * len(scalars) + [anywhere] * len(operands),
        out_specs=[anywhere] * len(out_pairs),
        scratch_shapes=list(scratch)
        + [pltpu.VMEM((count, 2) + slot, arrays[0].dtype)]
        + [pltpu.SemaphoreType.DMA((count,))] * 2,
        input_output_aliases={} if into is None else {len(scalars) + len(operands) - 1: 0},
        compiler_params=pltpu.CompilerParams(vmem_limit_bytes=size + 1024 * 1024),
        cost_estimate=BRIEF,
        name=name,
    )(*scalars, *operands)


def shifted(value, side, distance, direction):
    tp = lax.axis_size("tp")
    pairs = []
    for inst in range(side * side):
        for part in range(tp):
            x, y = inst % side, inst // side
            if (part % 2) ^ direction:
                y = (y + distance) % side
            else:
                x = (x + distance) % side
            pairs.append((inst * tp + part, (y * side + x) * tp + part))
    return lax.ppermute(value, ("inst", "tp"), pairs)


def attend_slots(start, group, meta_ref, len_ref, q_ref, kv_ref, max_ref, total_ref, sum_ref):
    step = pl.program_id(0)
    heads, width = q_ref.shape[1:]
    block = kv_ref.shape[3]
    lane = lax.broadcasted_iota(jnp.int32, (heads, block), 1)
    for j in range(group):
        at = step * group + j
        slot = start + at
        row = meta_ref[2 * slot]
        left = len_ref[row] - meta_ref[2 * slot + 1] * block
        scores = lax.dot_general(
            q_ref[row], kv_ref[j, 0, 0], (((1,), (1,)), ((), ())), preferred_element_type=jnp.float32
        ) * width ** (-0.5)
        valid = lane < left
        scores = jnp.where(valid, scores, LOWEST)
        peak = scores.max(-1, keepdims=True)
        weight = jnp.where(valid, jnp.exp(scores - peak), 0.0)
        high = weight.astype(jnp.bfloat16)
        low = (weight - high.astype(jnp.float32)).astype(jnp.bfloat16)
        both = jnp.dot(
            jnp.concatenate([high, low], axis=0), kv_ref[j, 1, 0], preferred_element_type=jnp.float32
        )
        sum_ref[at] = both[:heads] + both[heads:]
        max_ref[at] = jnp.broadcast_to(peak, (heads, width))
        total_ref[at] = jnp.broadcast_to(weight.sum(-1, keepdims=True), (heads, width))


def attend_early(group, meta_ref, len_ref, q_ref, kv_ref, max_ref, total_ref, sum_ref):
    attend_slots(0, group, meta_ref, len_ref, q_ref, kv_ref, max_ref, total_ref, sum_ref)


def attend_late(slots, start, group, meta_ref, len_ref, new_slot_ref, q_ref, kv_ref, *refs):
    early, out_ref, late = refs[:3], refs[3], refs[4:]
    attend_slots(start, group, meta_ref, len_ref, q_ref, kv_ref, *late)

    @pl.when(pl.program_id(0) == (slots - start) // group - 1)
    def _():
        rows, heads, width = q_ref.shape
        lanes = lax.broadcasted_iota(jnp.int32, (heads, width), 1)
        per = out_ref.shape[2] // width - 1

        def of_slot(slot):
            return [ref[slot] for ref in early] if slot < start else [ref[slot - start] for ref in late]

        for row in range(rows):
            peak = jnp.full((heads, width), LOWEST, jnp.float32)
            for slot in range(slots):
                peak = jnp.maximum(peak, jnp.where(meta_ref[2 * slot] == row, of_slot(slot)[0], LOWEST))
            total = jnp.zeros((heads, width), jnp.float32)
            summed = jnp.zeros((heads, width), jnp.float32)
            for slot in range(slots):
                slot_max, slot_total, slot_sum = of_slot(slot)
                scale = jnp.where(meta_ref[2 * slot] == row, jnp.exp(slot_max - peak), 0.0)
                total = total + scale * slot_total
                summed = summed + scale * slot_sum
            own = lax.broadcasted_iota(jnp.int32, (heads, width), 0) % per
            stats = jnp.where(lanes == MAX_LANE + own, peak, 0.0) + jnp.where(lanes == TOTAL_LANE + own, total, 0.0)
            for part in range(heads // per):
                dest = row * (heads // per) + part
                for n in range(per):
                    at = part * per + n
                    out_ref[dest, :, n * width : (n + 1) * width] = summed[at : at + 1]
                out_ref[dest, :, per * width :] = stats[part * per : (part + 1) * per].sum(0, keepdims=True)
        lanes = lax.broadcasted_iota(jnp.int32, (1, width), 1)
        for k in range(slots // 2):
            dest = new_slot_ref[2 * k] // slots
            values = [k] + [meta_ref[4 * k + n] for n in range(4)]
            tile = out_ref[dest, :, per * width :]
            for n, value in enumerate(values):
                value = jnp.full((1, width), value, jnp.int32).astype(jnp.float32)
                tile = jnp.where(lanes == META_LANE + n, value, tile)
            out_ref[dest, :, per * width :] = tile


def local(queries, kv_cache, slot_meta, row_len, new_slot, master):
    slots = kv_cache.shape[0]
    pairs = slots // 2
    side = math.isqrt(pairs)
    rows, heads, width = queries.shape
    per = rows * heads // pairs
    me = lax.axis_index("inst")

    kv_cache, new_slot = (pltpu.with_memory_space_constraint(array, pltpu.HBM) for array in (kv_cache, new_slot))
    order = pltpu.SMEM((pairs,), jnp.int32)

    def gathered(*hops):
        plan = functools.partial(gather_plan, hops, side, slots)
        return move(
            plan, len(hops) * side, [new_slot], [kv_cache], [side] * len(hops), "gather", scratch=[order]
        )

    def placed(arrays, pieces, into=None):
        plan = functools.partial(place_plan, pieces, side, len(arrays))
        scratch = [order, pltpu.SemaphoreType.DMA]
        return move(plan, len(pieces), [], arrays + [where], [pairs], "place", into=into, scratch=scratch)[0]

    turns = (2, 1, 3)
    (out_two,) = gathered(2)
    got_two = shifted(out_two, side, 2, 0)
    out_one, out_three = gathered(1, 3)
    got_one = shifted(out_one, side, 1, 0)
    got_three = shifted(out_three, side, 3, 0)
    queries, out_one = lax.optimization_barrier((queries, out_one))

    group = 4
    start = 20 // group * group
    whole = pl.BlockSpec((rows, heads, width), lambda i, *_: (0, 0, 0))
    partial = [jax.ShapeDtypeStruct((start, heads, width), jnp.float32)] * 3
    partial_specs = [pl.BlockSpec((start, heads, width), lambda i, *_: (0, 0, 0))] * 3
    params = pltpu.CompilerParams(dimension_semantics=("arbitrary",), vmem_limit_bytes=8 * 1024 * 1024)
    meta = slot_meta.reshape(-1)
    early = pl.pallas_call(
        functools.partial(attend_early, group),
        out_shape=partial,
        grid_spec=pltpu.PrefetchScalarGridSpec(
            num_scalar_prefetch=2,
            grid=(start // group,),
            in_specs=[whole, pl.BlockSpec((group,) + kv_cache.shape[1:], lambda i, *_: (i, 0, 0, 0, 0))],
            out_specs=partial_specs,
        ),
        compiler_params=params,
        cost_estimate=BRIEF,
        name="attend_early",
    )(meta, row_len, queries, kv_cache)
    early, got_two = lax.optimization_barrier((early, got_two))
    parts = pl.pallas_call(
        functools.partial(attend_late, slots, start, group),
        out_shape=jax.ShapeDtypeStruct((pairs, 1, (per + 1) * width), jnp.float32),
        grid_spec=pltpu.PrefetchScalarGridSpec(
            num_scalar_prefetch=3,
            grid=((slots - start) // group,),
            in_specs=[
                whole,
                pl.BlockSpec((group,) + kv_cache.shape[1:], lambda i, *_: (i + start // group, 0, 0, 0, 0)),
            ]
            + partial_specs,
            out_specs=pl.BlockSpec((pairs, 1, (per + 1) * width), lambda i, *_: (0, 0, 0)),
            scratch_shapes=[pltpu.VMEM((slots - start, heads, width), jnp.float32)] * 3,
        ),
        compiler_params=params,
        cost_estimate=BRIEF,
        name="attend_late",
    )(meta, row_len, new_slot, queries, kv_cache, *early)
    got_two, parts = lax.optimization_barrier((got_two, parts))
    plan = functools.partial(stage_plan, turns, side, slots)
    out_early = move(plan, 6, [new_slot], [kv_cache, got_two], [2] * 3, "stage", scratch=[order])
    got_early = [shifted(array, side, turn, 1) for array, turn in zip(out_early, turns)]
    mine = lax.all_to_all(parts, "inst", split_axis=0, concat_axis=0, tiled=True)
    got_one, got_three, out_early = lax.optimization_barrier((got_one, got_three, out_early))
    plan = functools.partial(split_plan, ((2, (0, 1)), (1, (0,)), (3, (0,)), (1, (1,)), (3, (1,))))
    out_late = move(plan, 6, [], [got_one, got_three], [2, 1, 1, 1, 1], "split")
    got_late = [shifted(out_late[0], side, 2, 1)]
    out_late, got_early = lax.optimization_barrier((out_late, got_early))
    got_late += [shifted(array, side, turn, 1) for array, turn in zip(out_late[1:3], turns[1:])]
    mine = mine.reshape(pairs, per + 1, width)
    details = mine[:, per, META_LANE : META_LANE + 5].astype(jnp.int32)
    where = details[:, 0]
    placing = where[None, :] == jnp.arange(pairs, dtype=jnp.int32)[:, None]
    moved_meta = jnp.sum(
        jnp.where(placing[:, :, None], details[None, :, 1:], 0), axis=1
    ).reshape(slots, 2)
    pieces = [(0, None, 0, 0), (1, 0, 2, 0), (2, 0, 1, 0), (3, 0, 3, 0)]
    pieces += [(4 + n, m, first, turn) for n, turn in enumerate(turns) for m, first in enumerate((0, 2))]
    moved_cache = placed([kv_cache, got_two, got_one, got_three] + got_early, pieces)

    out_last, got_late[0], moved_cache = lax.optimization_barrier((out_late[3:], got_late[0], moved_cache))
    got_last = [shifted(array, side, turn, 1) for array, turn in zip(out_last, turns[1:])]

    peaks = mine[:, per, MAX_LANE : MAX_LANE + per, None]
    totals = mine[:, per, TOTAL_LANE : TOTAL_LANE + per, None]
    scale = jnp.exp(peaks - peaks.max(0, keepdims=True))
    done = jnp.sum(mine[:, :per] * scale, axis=0) / jnp.sum(totals * scale, axis=0)
    everyone = jnp.broadcast_to(done[None], (pairs,) + done.shape)
    result = lax.all_to_all(everyone, "inst", split_axis=0, concat_axis=0, tiled=True)
    result = result.reshape(1, rows, heads, width)
    pieces = [(0, 0, 1, 2), (0, 1, 3, 2), (1, 0, 1, 1), (2, 0, 1, 3)]
    moved_cache = placed(got_late, pieces, moved_cache)
    attended = jnp.where((master == me)[None, :, None, None], result, jnp.float32(0.0))
    moved_cache = placed(got_last, [(0, 0, 3, 1), (1, 0, 3, 3)], moved_cache)
    return (moved_cache, moved_meta, attended)


def solution(mesh):
    in_specs = (
        P(None, "tp", None),
        P("inst", None, "tp", None, None),
        P("inst", None),
        P(),
        P("inst"),
        P(),
    )
    out_specs = (P("inst", None, "tp", None, None), P("inst", None), P("inst", None, "tp", None))
    return jax.shard_map(local, mesh=mesh, in_specs=in_specs, out_specs=out_specs, check_vma=False)
```

```python
import functools
import math

import jax
import jax.numpy as jnp
from jax import lax
from jax.experimental import pallas as pl
from jax.experimental.pallas import tpu as pltpu
from jax.sharding import PartitionSpec as P

LOWEST = -1e30
BRIEF = pl.CostEstimate(flops=1, bytes_accessed=1, transcendentals=0)
MAX_LANE, TOTAL_LANE, META_LANE = 0, 32, 64


def bits(size):
    assert size & (size - 1) == 0
    return size.bit_length() - 1


def coordinates(inst, side):
    crossed = lax.axis_index("tp") % 2 == 1
    x, y = inst & (side - 1), lax.shift_right_logical(inst, bits(side))
    return jnp.where(crossed, y, x), jnp.where(crossed, x, y)


def instance(first, second, side):
    crossed = lax.axis_index("tp") % 2 == 1
    return jnp.where(crossed, first * side + second, second * side + first)


def by_distance(side, slots, new_slot_ref, order):
    here = lax.axis_index("inst")
    x, y = here & (side - 1), lax.shift_right_logical(here, bits(side))
    for k in range(side * side):
        there = lax.shift_right_logical(new_slot_ref[2 * k], bits(slots))
        across = (there - x) & (side - 1)
        order[((lax.shift_right_logical(there, bits(side)) - y) & (side - 1)) * side + across] = k
    return lambda first, second: order[instance(first, second, side)]


def known_already():
    pass


def gather_plan(hops, side, slots, new_slot_ref, in_refs, out_refs, order):
    pair = by_distance(side, slots, new_slot_ref, order)
    pieces = [
        ((in_refs[0], pair(first, second)), (out, second))
        for out, first in zip(out_refs, hops)
        for second in range(side)
    ]
    return pieces, known_already


def stage_plan(turns, side, slots, new_slot_ref, in_refs, out_refs, order):
    pair = by_distance(side, slots, new_slot_ref, order)
    pieces = [
        ((ref, turn if n else pair(0, turn)), (out, n))
        for out, turn in zip(out_refs, turns)
        for n, ref in enumerate(in_refs)
    ]
    return pieces, known_already


def split_plan(parts, in_refs, out_refs):
    pieces = [
        ((in_refs[ref], turn), (out, n)) for out, (turn, refs) in zip(out_refs, parts) for n, ref in enumerate(refs)
    ]
    return pieces, known_already


def place_plan(pieces, side, where_at, in_refs, out_refs, where, sem):
    first_here, second_here = coordinates(lax.axis_index("inst"), side)
    fetch = pltpu.make_async_copy(in_refs[where_at], where, sem)
    fetch.start()
    plan = []
    for source, pair, first, second in pieces:
        origin = instance(
            (first_here - first) & (side - 1), (second_here - second) & (side - 1), side
        )
        target = functools.partial(where.__getitem__, origin)
        plan.append(((in_refs[source], target if pair is None else pair), (out_refs[0], target)))
    return plan, fetch.wait


def move_kernel(plan, n_scalars, n_in, n_out, *refs):
    scalars, in_refs = refs[:n_scalars], refs[n_scalars : n_scalars + n_in]
    out_refs, scratch = refs[n_scalars + n_in :][:n_out], refs[n_scalars + n_in + n_out :]
    *scratch, buffer, in_sems, out_sems = scratch
    pieces, known = plan(*scalars, in_refs, out_refs, *scratch)

    def part(ref, pair):
        return ref.at[pl.ds(2 * (pair() if callable(pair) else pair), 2)]

    def load(n):
        copy = pltpu.make_async_copy(part(*pieces[n][0]), buffer.at[n], in_sems.at[n])
        copy.start()
        return copy

    loads = [None if callable(pair) else load(n) for n, ((_, pair), _) in enumerate(pieces)]
    known()
    loads = [copy or load(n) for n, copy in enumerate(loads)]
    stores = []
    for n, copy in enumerate(loads):
        copy.wait()
        stores.append(pltpu.make_async_copy(buffer.at[n], part(*pieces[n][1]), out_sems.at[n]))
        stores[-1].start()
    for copy in stores:
        copy.wait()


def move(plan, count, scalars, arrays, out_pairs, name, into=None, scratch=()):
    slot = arrays[0].shape[1:]
    operands = arrays + ([] if into is None else [into])
    smem, anywhere = pl.BlockSpec(memory_space=pltpu.SMEM), pl.BlockSpec(memory_space=pl.ANY)
    size = count * 2 * math.prod(slot) * arrays[0].dtype.itemsize
    return pl.pallas_call(
        functools.partial(move_kernel, plan, len(scalars), len(operands), len(out_pairs)),
        out_shape=[pltpu.HBM((2 * n,) + slot, arrays[0].dtype) for n in out_pairs],
        in_specs=[smem] * len(scalars) + [anywhere] * len(operands),
        out_specs=[anywhere] * len(out_pairs),
        scratch_shapes=list(scratch)
        + [pltpu.VMEM((count, 2) + slot, arrays[0].dtype)]
        + [pltpu.SemaphoreType.DMA((count,))] * 2,
        input_output_aliases={} if into is None else {len(scalars) + len(operands) - 1: 0},
        compiler_params=pltpu.CompilerParams(vmem_limit_bytes=size + 1024 * 1024),
        cost_estimate=BRIEF,
        name=name,
    )(*scalars, *operands)


def shifted(value, side, distance, direction):
    tp = lax.axis_size("tp")
    pairs = []
    for inst in range(side * side):
        for part in range(tp):
            x, y = inst % side, inst // side
            if (part % 2) ^ direction:
                y = (y + distance) % side
            else:
                x = (x + distance) % side
            pairs.append((inst * tp + part, (y * side + x) * tp + part))
    return lax.ppermute(value, ("inst", "tp"), pairs)


def attend_slots(start, group, meta_ref, len_ref, q_ref, kv_ref, max_ref, total_ref, sum_ref):
    step = pl.program_id(0)
    heads, width = q_ref.shape[1:]
    block = kv_ref.shape[3]
    lane = lax.broadcasted_iota(jnp.int32, (heads, block), 1)
    for j in range(group):
        at = step * group + j
        slot = start + at
        row = meta_ref[2 * slot]
        left = len_ref[row] - meta_ref[2 * slot + 1] * block
        scores = lax.dot_general(
            q_ref[row], kv_ref[j, 0, 0], (((1,), (1,)), ((), ())), preferred_element_type=jnp.float32
        ) * width ** (-0.5)
        valid = lane < left
        scores = jnp.where(valid, scores, LOWEST)
        peak = scores.max(-1, keepdims=True)
        weight = jnp.where(valid, jnp.exp(scores - peak), 0.0)
        high = weight.astype(jnp.bfloat16)
        low = (weight - high.astype(jnp.float32)).astype(jnp.bfloat16)
        both = jnp.dot(
            jnp.concatenate([high, low], axis=0), kv_ref[j, 1, 0], preferred_element_type=jnp.float32
        )
        sum_ref[at] = both[:heads] + both[heads:]
        max_ref[at] = jnp.broadcast_to(peak, (heads, width))
        total_ref[at] = jnp.broadcast_to(weight.sum(-1, keepdims=True), (heads, width))


def attend_early(group, meta_ref, len_ref, q_ref, kv_ref, max_ref, total_ref, sum_ref):
    attend_slots(0, group, meta_ref, len_ref, q_ref, kv_ref, max_ref, total_ref, sum_ref)


def attend_late(slots, start, group, meta_ref, len_ref, new_slot_ref, q_ref, kv_ref, *refs):
    early, out_ref, late = refs[:3], refs[3], refs[4:]
    attend_slots(start, group, meta_ref, len_ref, q_ref, kv_ref, *late)

    @pl.when(pl.program_id(0) == (slots - start) // group - 1)
    def _():
        rows, heads, width = q_ref.shape
        lanes = lax.broadcasted_iota(jnp.int32, (heads, width), 1)
        per = out_ref.shape[2] // width - 1

        def of_slot(slot):
            return [ref[slot] for ref in early] if slot < start else [ref[slot - start] for ref in late]

        for row in range(rows):
            peak = jnp.full((heads, width), LOWEST, jnp.float32)
            for slot in range(slots):
                peak = jnp.maximum(peak, jnp.where(meta_ref[2 * slot] == row, of_slot(slot)[0], LOWEST))
            total = jnp.zeros((heads, width), jnp.float32)
            summed = jnp.zeros((heads, width), jnp.float32)
            for slot in range(slots):
                slot_max, slot_total, slot_sum = of_slot(slot)
                scale = jnp.where(meta_ref[2 * slot] == row, jnp.exp(slot_max - peak), 0.0)
                total = total + scale * slot_total
                summed = summed + scale * slot_sum
            own = lax.broadcasted_iota(jnp.int32, (heads, width), 0) % per
            stats = jnp.where(lanes == MAX_LANE + own, peak, 0.0) + jnp.where(lanes == TOTAL_LANE + own, total, 0.0)
            for part in range(heads // per):
                dest = row * (heads // per) + part
                for n in range(per):
                    at = part * per + n
                    out_ref[dest, :, n * width : (n + 1) * width] = summed[at : at + 1]
                out_ref[dest, :, per * width :] = stats[part * per : (part + 1) * per].sum(0, keepdims=True)
        lanes = lax.broadcasted_iota(jnp.int32, (1, width), 1)
        for k in range(slots // 2):
            dest = new_slot_ref[2 * k] // slots
            values = [k] + [meta_ref[4 * k + n] for n in range(4)]
            tile = out_ref[dest, :, per * width :]
            for n, value in enumerate(values):
                value = jnp.full((1, width), value, jnp.int32).astype(jnp.float32)
                tile = jnp.where(lanes == META_LANE + n, value, tile)
            out_ref[dest, :, per * width :] = tile


def local(queries, kv_cache, slot_meta, row_len, new_slot, master):
    slots = kv_cache.shape[0]
    pairs = slots // 2
    side = math.isqrt(pairs)
    rows, heads, width = queries.shape
    per = rows * heads // pairs
    me = lax.axis_index("inst")

    kv_cache, new_slot = (pltpu.with_memory_space_constraint(array, pltpu.HBM) for array in (kv_cache, new_slot))
    order = pltpu.SMEM((pairs,), jnp.int32)

    def gathered(*hops):
        plan = functools.partial(gather_plan, hops, side, slots)
        return move(
            plan, len(hops) * side, [new_slot], [kv_cache], [side] * len(hops), "gather", scratch=[order]
        )

    def placed(arrays, pieces, into=None):
        plan = functools.partial(place_plan, pieces, side, len(arrays))
        scratch = [order, pltpu.SemaphoreType.DMA]
        return move(plan, len(pieces), [], arrays + [where], [pairs], "place", into=into, scratch=scratch)[0]

    turns = (2, 1, 3)
    (out_two,) = gathered(2)
    got_two = shifted(out_two, side, 2, 0)
    out_one, out_three = gathered(1, 3)
    got_one = shifted(out_one, side, 1, 0)
    got_three = shifted(out_three, side, 3, 0)
    queries, out_one = lax.optimization_barrier((queries, out_one))

    group = 8
    start = 16 // group * group
    whole = pl.BlockSpec((rows, heads, width), lambda i, *_: (0, 0, 0))
    partial = [jax.ShapeDtypeStruct((start, heads, width), jnp.float32)] * 3
    partial_specs = [pl.BlockSpec((start, heads, width), lambda i, *_: (0, 0, 0))] * 3
    params = pltpu.CompilerParams(dimension_semantics=("arbitrary",), vmem_limit_bytes=8 * 1024 * 1024)
    meta = slot_meta.reshape(-1)
    early = pl.pallas_call(
        functools.partial(attend_early, group),
        out_shape=partial,
        grid_spec=pltpu.PrefetchScalarGridSpec(
            num_scalar_prefetch=2,
            grid=(start // group,),
            in_specs=[whole, pl.BlockSpec((group,) + kv_cache.shape[1:], lambda i, *_: (i, 0, 0, 0, 0))],
            out_specs=partial_specs,
        ),
        compiler_params=params,
        cost_estimate=BRIEF,
        name="attend_early",
    )(meta, row_len, queries, kv_cache)
    early, got_two = lax.optimization_barrier((early, got_two))
    parts = pl.pallas_call(
        functools.partial(attend_late, slots, start, group),
        out_shape=jax.ShapeDtypeStruct((pairs, 1, (per + 1) * width), jnp.float32),
        grid_spec=pltpu.PrefetchScalarGridSpec(
            num_scalar_prefetch=3,
            grid=((slots - start) // group,),
            in_specs=[
                whole,
                pl.BlockSpec((group,) + kv_cache.shape[1:], lambda i, *_: (i + start // group, 0, 0, 0, 0)),
            ]
            + partial_specs,
            out_specs=pl.BlockSpec((pairs, 1, (per + 1) * width), lambda i, *_: (0, 0, 0)),
            scratch_shapes=[pltpu.VMEM((slots - start, heads, width), jnp.float32)] * 3,
        ),
        compiler_params=params,
        cost_estimate=BRIEF,
        name="attend_late",
    )(meta, row_len, new_slot, queries, kv_cache, *early)
    got_two, parts = lax.optimization_barrier((got_two, parts))
    plan = functools.partial(stage_plan, turns, side, slots)
    out_early = move(plan, 6, [new_slot], [kv_cache, got_two], [2] * 3, "stage", scratch=[order])
    got_early = [shifted(array, side, turn, 1) for array, turn in zip(out_early, turns)]
    mine = lax.all_to_all(parts, "inst", split_axis=0, concat_axis=0, tiled=True)
    got_one, got_three, out_early = lax.optimization_barrier((got_one, got_three, out_early))
    plan = functools.partial(split_plan, ((2, (0, 1)), (1, (0,)), (3, (0,)), (1, (1,)), (3, (1,))))
    out_late = move(plan, 6, [], [got_one, got_three], [2, 1, 1, 1, 1], "split")
    got_late = [shifted(out_late[0], side, 2, 1)]
    out_late, got_early = lax.optimization_barrier((out_late, got_early))
    got_late += [shifted(array, side, turn, 1) for array, turn in zip(out_late[1:3], turns[1:])]
    mine = mine.reshape(pairs, per + 1, width)
    details = mine[:, per, META_LANE : META_LANE + 5].astype(jnp.int32)
    where = details[:, 0]
    placing = where[None, :] == jnp.arange(pairs, dtype=jnp.int32)[:, None]
    moved_meta = jnp.sum(
        jnp.where(placing[:, :, None], details[None, :, 1:], 0), axis=1
    ).reshape(slots, 2)
    pieces = [(0, None, 0, 0), (1, 0, 2, 0), (2, 0, 1, 0), (3, 0, 3, 0)]
    pieces += [(4 + n, m, first, turn) for n, turn in enumerate(turns) for m, first in enumerate((0, 2))]
    moved_cache = placed([kv_cache, got_two, got_one, got_three] + got_early, pieces)

    out_last, got_late[0], moved_cache = lax.optimization_barrier((out_late[3:], got_late[0], moved_cache))
    got_last = [shifted(array, side, turn, 1) for array, turn in zip(out_last, turns[1:])]

    peaks = mine[:, per, MAX_LANE : MAX_LANE + per, None]
    totals = mine[:, per, TOTAL_LANE : TOTAL_LANE + per, None]
    scale = jnp.exp(peaks - peaks.max(0, keepdims=True))
    done = jnp.sum(mine[:, :per] * scale, axis=0) / jnp.sum(totals * scale, axis=0)
    everyone = jnp.broadcast_to(done[None], (pairs,) + done.shape)
    result = lax.all_to_all(everyone, "inst", split_axis=0, concat_axis=0, tiled=True)
    result = result.reshape(1, rows, heads, width)
    pieces = [(0, 0, 1, 2), (0, 1, 3, 2), (1, 0, 1, 1), (2, 0, 1, 3)]
    moved_cache = placed(got_late, pieces, moved_cache)
    attended = jnp.where((master == me)[None, :, None, None], result, jnp.float32(0.0))
    moved_cache = placed(got_last, [(0, 0, 3, 1), (1, 0, 3, 3)], moved_cache)
    return (moved_cache, moved_meta, attended)


def solution(mesh):
    in_specs = (
        P(None, "tp", None),
        P("inst", None, "tp", None, None),
        P("inst", None),
        P(),
        P("inst"),
        P(),
    )
    out_specs = (P("inst", None, "tp", None, None), P("inst", None), P("inst", None, "tp", None))
    return jax.shard_map(local, mesh=mesh, in_specs=in_specs, out_specs=out_specs, check_vma=False)
```
